32 devices in a mesh: dp: 2 (over x), seq: 16 (over z, y, core).
Axes of the slice: x: 2, y: 2, z: 4, core: 2. Of those that a mesh axis runs over, the one named last changes fastest.
Arguments:
- inputs: bfloat16 [64, 256, 1024], P('seq', 'dp'), may hold values from -6 to 6
- gates: bfloat16 [64, 256, 1024], P('seq', 'dp'), may hold values from -6 to 6
- kernel: bfloat16 [64, 256, 1024], P('seq', 'dp'), may hold values from -5 to 5
- first_factor: bfloat16 [1024, 1024], replicated, may hold values from -0.1875 to 0.1875
- second_factor: bfloat16 [64, 64], replicated, may hold values from -0.75 to 0.75
- upstream: bfloat16 [64, 256, 1024], P('seq', 'dp'), may hold values from -6 to 6
Outputs:
- output: bfloat16 [64, 256, 1024], P('seq', 'dp')
- grad_inputs: bfloat16 [64, 256, 1024], P('seq', 'dp')
- grad_gates: bfloat16 [64, 256, 1024], P('seq', 'dp')
- grad_kernel: bfloat16 [64, 256, 1024], P('seq', 'dp')
- grad_first: float32 [1024, 1024], P('seq')
- grad_second: float32 [64, 64], P('seq')
The draws below stay inside these ranges and needn't reach their ends.
All inputs are finite; a program needn't handle non-finite values.
Results may differ from the reference program's by a relative error of at most 0.0065.
Values may be sent and summed in bfloat16 or wider, within the bound.
A program may use at most 64 MiB of HBM per device.

```python
import math
import jax
import jax.numpy as jnp

BS = 1024
NB = 64
C = 256


def block_scale(rng, extent, split, smallest, largest):
    level, own = 1.0, jax.random.fold_in(rng, 6)
    for axis_at, parts in split:
        heights = jnp.exp(jax.random.uniform(jax.random.fold_in(own, axis_at), (parts,), jnp.float32, smallest / len(split), largest / len(split)))
        level = level * jnp.repeat(heights, extent[axis_at] // parts).reshape([-1 if axis == axis_at else 1 for axis in range(len(extent))])
    return level


def bell_draw(rng, shape, scale, limit, split=(), kind=jnp.bfloat16):
    factor_of = block_scale(rng, shape, split, -0.22, 0.18) if split else 1.0
    values = jax.random.normal(rng, shape, jnp.float32) * scale * factor_of
    return jnp.minimum(jnp.maximum(values, -limit), limit).astype(kind)


def setup_inputs(seed: int = 0) -> dict:
    splits = jax.random.split(jax.random.key(seed), 7)
    inputs = bell_draw(splits[0], (NB, C, BS), 1.0, 6.0, ((0, 16), (1, 2)))
    gates = bell_draw(splits[1], (NB, C, BS), 1.5, 6.0, ((0, 16), (1, 2)))
    kernel = bell_draw(splits[2], (NB, C, BS), 1.0, 5.0, ((0, 16), (1, 2)))
    first_factor = bell_draw(splits[3], (BS, BS), BS ** -0.5, 0.1875)
    second_factor = bell_draw(splits[4], (NB, NB), NB ** -0.5, 0.75)
    upstream = bell_draw(splits[5], (NB, C, BS), 1.0, 6.0, ((0, 16), (1, 2)))
    return dict(inputs=inputs, gates=gates, kernel=kernel, first_factor=first_factor, second_factor=second_factor, upstream=upstream)


def reference(inputs, gates, kernel, first_factor, second_factor, upstream):
    sig = jax.nn.sigmoid(gates.astype(jnp.float32))
    mixed_in = (inputs.astype(jnp.float32) * sig).astype(jnp.bfloat16)
    flat_in = mixed_in.reshape(NB * C, BS)
    blocks = jnp.dot(flat_in, first_factor.T, preferred_element_type=jnp.float32).astype(jnp.bfloat16).reshape(NB, C, BS)
    kerneled = (blocks.astype(jnp.float32) * kernel.astype(jnp.float32)).astype(jnp.bfloat16)
    flat_kern = kerneled.reshape(NB, C * BS)
    output = jnp.dot(second_factor, flat_kern, preferred_element_type=jnp.float32).astype(jnp.bfloat16).reshape(NB, C, BS)
    flat_up = upstream.reshape(NB, C * BS)
    grad_mid = jnp.dot(second_factor.T, flat_up, preferred_element_type=jnp.float32).astype(jnp.bfloat16).reshape(NB, C, BS)
    grad_kernel = (grad_mid.astype(jnp.float32) * blocks.astype(jnp.float32)).astype(jnp.bfloat16)
    grad_blocks = (grad_mid.astype(jnp.float32) * kernel.astype(jnp.float32)).astype(jnp.bfloat16)
    flat_grad = grad_blocks.reshape(NB * C, BS)
    grad_mixed = jnp.dot(flat_grad, first_factor, preferred_element_type=jnp.float32).reshape(NB, C, BS)
    grad_inputs = (grad_mixed * sig).astype(jnp.bfloat16)
    grad_gates = (grad_mixed * inputs.astype(jnp.float32) * sig * (1.0 - sig)).astype(jnp.bfloat16)
    grad_first = jnp.dot(flat_grad.T, flat_in, preferred_element_type=jnp.float32) / math.sqrt(NB * C)
    grad_second = jnp.dot(flat_up, flat_kern.T, preferred_element_type=jnp.float32) / math.sqrt(C * BS)
    return (output, grad_inputs, grad_gates, grad_kernel, grad_first, grad_second)
```

```python
import functools
import math

import jax
import jax.numpy as jnp
from jax import lax
from jax.experimental import pallas as pl
from jax.experimental.pallas import tpu as pltpu
from jax.sharding import PartitionSpec as P

MESH = pl.DeviceIdType.MESH
BF = jnp.bfloat16
F32 = jnp.float32
CS = 16


def dot(a, b, ca, cb, **kw):
    return lax.dot_general(a, b, (((ca,), (cb,)), ((), ())), preferred_element_type=F32, **kw)


def layer_kernel(
    n, dps, lb, ch, w, nb,
    x_hbm, g_hbm, k_hbm, f_hbm, s_ref, u_hbm,
    out_hbm, gi_hbm, gg_hbm, gk_hbm, gf_ref, gs_ref,
    x, g, k, f, mixed, blocks, kern, mu, mk, gac, oac, gm, om, gb, gi, gg, gk,
    kron, kron_t, gf, rs_send, rs_recv, dpbuf, g2s, g2r, g2dp,
    load_sem, own_sem, store_sem, send_sem, recv_sem, rs_ssem, rs_rsem,
    g2_ssem, g2_rsem, dp_ssem, dp_rsem,
):
    me = lax.axis_index("seq")
    my_dp = lax.axis_index("dp")
    pg = n // (ch // CS)
    pw = w // pg
    rows = nb * CS
    step_rows = 4 * lb * CS
    steps = n // 4
    owned = w // n
    levels = n.bit_length() - 1

    def share(ref, d):
        c0 = pl.multiple_of(lax.div(d, pg) * CS, CS)
        p0 = pl.multiple_of(lax.rem(d, pg) * pw, pw)
        return ref.at[:, pl.ds(c0, CS), pl.ds(p0, pw)]

    def part(ref, d):
        return ref.at[pl.ds(d * lb, lb)]

    def copy_to(phase, src, dst, d, s):
        return pltpu.make_async_remote_copy(
            src_ref=src, dst_ref=dst,
            send_sem=send_sem.at[phase, d], recv_sem=recv_sem.at[phase, s],
            device_id={"seq": d}, device_id_type=MESH,
        )

    loads = [
        pltpu.make_async_copy(a, b, load_sem.at[i])
        for i, (a, b) in enumerate(((g_hbm, g), (x_hbm, x), (f_hbm, f), (k_hbm, k)))
    ]
    for c in loads:
        c.start()
    own_u = pltpu.make_async_copy(share(u_hbm, me), part(mu, me), own_sem.at[0])
    own_u.start()

    barrier = pltpu.get_barrier_semaphore()

    @pl.loop(1, n)
    def _(j):
        pl.semaphore_signal(
            barrier, inc=1, device_id={"seq": lax.rem(me + j, n)}, device_id_type=MESH
        )

    for j in range(1, dps):
        pl.semaphore_signal(
            barrier, inc=1, device_id={"dp": lax.rem(my_dp + j, dps)}, device_id_type=MESH
        )
    pl.semaphore_wait(barrier, n - 1 + dps - 1)

    @pl.loop(1, n)
    def _(j):
        d = lax.rem(me + j, n)
        copy_to(0, share(u_hbm, d), part(mu, me), d, me).start()

    for c in loads:
        c.wait()

    @pl.loop(0, lb)
    def _(i):
        sig = jax.nn.sigmoid(g[i].astype(F32))
        mixed[i] = (x[i].astype(F32) * sig).astype(BF)

    @pl.loop(0, w // 256)
    def _(j):
        cols = pl.ds(pl.multiple_of(j * 256, 256), 256)
        b = dot(mixed[...].reshape(lb * ch, w), f[cols, :], 1, 1)
        b = b.astype(BF).reshape(lb, ch, 256)
        blocks[:, :, cols] = b
        kern[:, :, cols] = (b.astype(F32) * k[:, :, cols].astype(F32)).astype(BF)

    def spread(r0, count, width):
        r = lax.broadcasted_iota(jnp.int32, (count, width), 0) + r0
        lo = lax.broadcasted_iota(jnp.int32, (count, width), 1) * CS
        return jnp.where((r >= lo) & (r < lo + CS), 1.0, 0.0)

    def same_channel():
        r = lax.broadcasted_iota(jnp.int32, (step_rows, rows), 0)
        c = lax.broadcasted_iota(jnp.int32, (step_rows, rows), 1)
        return (r & (CS - 1)) == (c & (CS - 1))

    def build(dst, dim):
        @pl.loop(0, steps)
        def _(j):
            r0 = pl.multiple_of(j * step_rows, step_rows)
            a = dot(spread(r0, step_rows, nb).astype(BF), s_ref[...], 1, dim).astype(BF)
            e = dot(a, spread(0, rows, nb).astype(BF), 1, 1)
            dst[pl.ds(r0, step_rows), :] = jnp.where(same_channel(), e, 0.0).astype(BF)

    build(kron_t, 1)
    build(kron, 0)

    def wait_in(phase, dst):
        @pl.loop(1, n)
        def _(j):
            s = lax.rem(me + j, n)
            copy_to(phase, part(dst, s), part(dst, s), s, s).wait_recv()

    def wait_back(phase, dst):
        @pl.loop(1, n)
        def _(j):
            s = lax.rem(me + j, n)
            copy_to(phase, share(dst, s), share(dst, s), s, s).wait_recv()

    def mix(phase, matrix, src, acc, dst, sem):
        @pl.loop(0, steps)
        def _(j):
            at = lax.rem(lax.div(me, 4) + j, steps)
            r0 = pl.multiple_of(at * step_rows, step_rows)
            res = dot(matrix[pl.ds(r0, step_rows), :], src[...].reshape(rows, pw), 1, 0)
            acc[pl.ds(at * 4 * lb, 4 * lb)] = res.astype(BF).reshape(4 * lb, CS, pw)

            @pl.loop(0, 4)
            def _(i):
                d = at * 4 + i

                @pl.when(d != me)
                def _():
                    copy_to(phase, part(acc, d), share(dst, me), d, me).start()

        own = pltpu.make_async_copy(part(acc, me), share(dst, me), sem)
        own.start()
        return own

    own_u.wait()
    wait_in(0, mu)
    own_g = mix(1, kron_t, mu, gac, gm, own_sem.at[1])

    own_k = pltpu.make_async_copy(share(kern, me), part(mk, me), own_sem.at[2])
    own_k.start()

    @pl.loop(1, n)
    def _(j):
        d = lax.rem(me + j, n)
        copy_to(2, share(kern, d), part(mk, me), d, me).start()

    own_g.wait()
    wait_back(1, gm)

    @pl.loop(0, lb)
    def _(i):
        mid = gm[i].astype(F32)
        gk[i] = (mid * blocks[i].astype(F32)).astype(BF)
        gb[i] = (mid * k[i].astype(F32)).astype(BF)

    gk_store = pltpu.make_async_copy(gk, gk_hbm, store_sem.at[0])
    gk_store.start()

    def place(owner):
        return sum(((owner >> b) & 1) * (w >> (b + 1)) for b in range(levels))

    for j in range(w // 256):
        cols = pl.ds(j * 256, 256)
        res = dot(gb[:, :, cols].reshape(lb * ch, 256), mixed[...].reshape(lb * ch, w), 0, 0)
        for i in range(256 // owned):
            gf[pl.ds(place(j * (256 // owned) + i), owned), :] = res[i * owned:(i + 1) * owned]

    base = 0
    offset = 0
    halves = []

    def half_start(level, base, offset):
        size = w >> (level + 1)
        bit = lax.rem(lax.div(me, 1 << level), 2)
        keep = pl.multiple_of(base + bit * size, owned)
        give = pl.multiple_of(base + (1 - bit) * size, owned)

        @pl.loop(0, size // owned)
        def _(i):
            to = pl.multiple_of(offset + i * owned, owned)
            rs_send[pl.ds(to, owned), :] = gf[pl.ds(give + i * owned, owned), :].astype(BF)

        copy = pltpu.make_async_remote_copy(
            src_ref=rs_send.at[pl.ds(offset, size)], dst_ref=rs_recv.at[pl.ds(offset, size)],
            send_sem=rs_ssem.at[level], recv_sem=rs_rsem.at[level],
            device_id={"seq": me + (1 - 2 * bit) * (1 << level)}, device_id_type=MESH,
        )
        copy.start()
        halves.append(copy)
        return keep, offset + size

    def half_end(level, keep, offset):
        size = w >> (level + 1)
        halves[level].wait_recv()

        @pl.loop(0, size // owned)
        def _(i):
            at = pl.ds(pl.multiple_of(keep + i * owned, owned), owned)
            come = pl.ds(pl.multiple_of(offset - size + i * owned, owned), owned)
            gf[at, :] = gf[at, :] + rs_recv[come, :].astype(F32)

    base, offset = half_start(0, base, offset)

    @pl.loop(0, lb)
    def _(i):
        gmx = dot(gb[i], f[...], 1, 0)
        sig = jax.nn.sigmoid(g[i].astype(F32))
        gi[i] = (gmx * sig).astype(BF)
        gg[i] = (gmx * x[i].astype(F32) * sig * (1.0 - sig)).astype(BF)

    gi_store = pltpu.make_async_copy(gi, gi_hbm, store_sem.at[1])
    gi_store.start()
    gg_store = pltpu.make_async_copy(gg, gg_hbm, store_sem.at[2])
    gg_store.start()

    half_end(0, base, offset)
    base, offset = half_start(1, base, offset)

    own_k.wait()
    wait_in(2, mk)
    own_o = mix(3, kron, mk, oac, om, own_sem.at[3])

    half_end(1, base, offset)
    base, offset = half_start(2, base, offset)

    lanes = g2s.shape[2]
    g2s[...] = jnp.zeros_like(g2s)
    for j in range(steps):
        part_u = mu[pl.ds(j * 4 * lb, 4 * lb)].reshape(step_rows, pw)
        h = dot(part_u, mk[...].reshape(rows, pw), 1, 1)
        h = jnp.where(same_channel(), h, 0.0).reshape(4 * lb, CS, rows).sum(axis=1)
        h = dot(h, spread(0, rows, lanes), 1, 0, precision=lax.Precision.HIGHEST)
        for i in range(4):
            g2s[j * 4 + i, 0:lb, :] = h[i * lb:(i + 1) * lb]

    def g2_copy(d, s):
        return pltpu.make_async_remote_copy(
            src_ref=g2s.at[d], dst_ref=g2r.at[s],
            send_sem=g2_ssem.at[d], recv_sem=g2_rsem.at[s],
            device_id={"seq": d}, device_id_type=MESH,
        )

    @pl.loop(1, n)
    def _(j):
        d = lax.rem(me + j, n)
        g2_copy(d, me).start()

    g2r[pl.ds(me, 1)] = g2s[pl.ds(me, 1)]

    for level in range(2, levels):
        half_end(level, base, offset)
        if level + 1 < levels:
            base, offset = half_start(level + 1, base, offset)

    @pl.loop(1, n)
    def _(j):
        s = lax.rem(me + j, n)
        g2_copy(s, s).wait_recv()

    dpbuf[pl.ds(my_dp, 1)] = gf[pl.ds(base, owned), :].astype(BF)[None]
    g2dp[pl.ds(my_dp, 1)] = jnp.sum(g2r[...], axis=0, keepdims=True)

    def dp_copies(d, s):
        return [
            pltpu.make_async_remote_copy(
                src_ref=buf.at[s], dst_ref=buf.at[s],
                send_sem=dp_ssem.at[i, d], recv_sem=dp_rsem.at[i, s],
                device_id={"dp": d}, device_id_type=MESH,
            )
            for i, buf in enumerate((dpbuf, g2dp))
        ]

    for j in range(1, dps):
        for c in dp_copies(lax.rem(my_dp + j, dps), my_dp):
            c.start()
    for j in range(1, dps):
        s = lax.rem(my_dp + j, dps)
        for c in dp_copies(s, s):
            c.wait_recv()
    first = dpbuf[0].astype(F32)
    second = g2dp[0]
    for i in range(1, dps):
        first = first + dpbuf[i].astype(F32)
        second = second + g2dp[i]
    gf_ref[...] = first * (1.0 / math.sqrt(nb * ch * dps))
    gs_ref[...] = second[0:lb, 0:nb] * (1.0 / math.sqrt(ch * dps * w))

    own_o.wait()
    wait_back(3, om)
    out_store = pltpu.make_async_copy(om, out_hbm, store_sem.at[3])
    out_store.start()

    @pl.loop(1, n)
    def _(j):
        d = lax.rem(me + j, n)
        copy_to(0, share(u_hbm, d), part(mu, me), d, me).wait_send()
        copy_to(1, part(gac, d), share(gm, me), d, me).wait_send()
        copy_to(2, share(kern, d), part(mk, me), d, me).wait_send()
        copy_to(3, part(oac, d), share(om, me), d, me).wait_send()
        g2_copy(d, me).wait_send()

    for c in halves:
        c.wait_send()
    for j in range(1, dps):
        for c in dp_copies(lax.rem(my_dp + j, dps), my_dp):
            c.wait_send()
    gk_store.wait()
    gi_store.wait()
    gg_store.wait()
    out_store.wait()


def on_device(n, dps, inputs, gates, kernel, first_factor, second_factor, upstream):
    lb, ch, w = inputs.shape
    nb = second_factor.shape[0]
    pw = w // (n // (ch // CS))
    owned = w // n
    levels = n.bit_length() - 1
    lanes = max(nb, 128)
    act = jax.ShapeDtypeStruct((lb, ch, w), BF)
    a_act = pltpu.VMEM((lb, ch, w), BF)
    a_mov = pltpu.VMEM((nb, CS, pw), BF)
    hbm = pl.BlockSpec(memory_space=pl.ANY)
    vmem = pl.BlockSpec(memory_space=pltpu.VMEM)
    sem = pltpu.SemaphoreType.DMA
    flops = 6 * lb * ch * w * w
    return pl.pallas_call(
        functools.partial(layer_kernel, n, dps, lb, ch, w, nb),
        out_shape=(
            act, act, act, act,
            jax.ShapeDtypeStruct((owned, w), F32),
            jax.ShapeDtypeStruct((lb, nb), F32),
        ),
        in_specs=[hbm, hbm, hbm, hbm, vmem, hbm],
        out_specs=(hbm, hbm, hbm, hbm, vmem, vmem),
        scratch_shapes=[
            a_act, a_act, a_act, pltpu.VMEM((w, w), BF),
            a_act, a_act, a_act,
            a_mov, a_mov, a_mov, a_mov,
            a_act, a_act, a_act, a_act, a_act, a_act,
            pltpu.VMEM((nb * CS, nb * CS), BF), pltpu.VMEM((nb * CS, nb * CS), BF),
            pltpu.VMEM((w, w), F32),
            pltpu.VMEM((w, w), BF), pltpu.VMEM((w, w), BF),
            pltpu.VMEM((dps, owned, w), BF),
            pltpu.VMEM((n, 8, lanes), F32), pltpu.VMEM((n, 8, lanes), F32),
            pltpu.VMEM((dps, 8, lanes), F32),
            sem((4,)), sem((4,)), sem((4,)), sem((4, n)), sem((4, n)),
            sem((levels,)), sem((levels,)), sem((n,)), sem((n,)), sem((2, dps)), sem((2, dps)),
        ],
        compiler_params=pltpu.CompilerParams(
            collective_id=0, has_side_effects=True, vmem_limit_bytes=58 * 1024 * 1024
        ),
        cost_estimate=pl.CostEstimate(flops=flops, bytes_accessed=10 << 20, transcendentals=0),
    )(inputs, gates, kernel, first_factor, second_factor, upstream)


def solution(mesh):
    cut = P("seq", "dp", None)
    return jax.shard_map(
        functools.partial(on_device, mesh.shape["seq"], mesh.shape["dp"]),
        mesh=mesh,
        in_specs=(cut, cut, cut, P(), P(), cut),
        out_specs=(cut, cut, cut, cut, P("seq", None), P("seq", None)),
        check_vma=False,
    )
```

```python
import functools
import math

import jax
import jax.numpy as jnp
from jax import lax
from jax.experimental import pallas as pl
from jax.experimental.pallas import tpu as pltpu
from jax.sharding import PartitionSpec as P

MESH = pl.DeviceIdType.MESH
BF = jnp.bfloat16
F32 = jnp.float32
CS = 16


def dot(a, b, ca, cb, **kw):
    return lax.dot_general(a, b, (((ca,), (cb,)), ((), ())), preferred_element_type=F32, **kw)


def layer_kernel(
    n, dps, lb, ch, w, nb,
    x_hbm, g_hbm, k_hbm, f_hbm, s_ref, u_hbm,
    out_hbm, gi_hbm, gg_hbm, gk_hbm, gf_ref, gs_ref,
    x, g, k, f, mixed, blocks, kern, mu, mk, gac, oac, gm, om, gb, gi, gg, gk,
    kron, kron_t, gf, rs_send, rs_recv, dpbuf, g2s, g2r, g2dp,
    load_sem, own_sem, store_sem, send_sem, recv_sem, rs_ssem, rs_rsem,
    g2_ssem, g2_rsem, dp_ssem, dp_rsem,
):
    me = lax.axis_index("seq")
    my_dp = lax.axis_index("dp")
    pg = n // (ch // CS)
    pw = w // pg
    rows = nb * CS
    step_rows = 4 * lb * CS
    steps = n // 4
    owned = w // n
    levels = n.bit_length() - 1

    hw = pw // 2

    def share(ref, d):
        c0 = pl.multiple_of(lax.div(d, pg) * CS, CS)
        p0 = pl.multiple_of(lax.rem(d, pg) * pw, pw)
        return ref.at[:, pl.ds(c0, CS), pl.ds(p0, pw)]

    def half_share(half, ref, d):
        c0 = pl.multiple_of(lax.div(d, pg) * CS, CS)
        p0 = pl.multiple_of(lax.rem(d, pg) * pw + half * hw, hw)
        return ref.at[:, pl.ds(c0, CS), pl.ds(p0, hw)]

    share_of = [functools.partial(half_share, i) for i in range(2)]

    def part(ref, d):
        return ref.at[pl.ds(d * lb, lb)]

    def copy_to(phase, src, dst, d, s):
        return pltpu.make_async_remote_copy(
            src_ref=src, dst_ref=dst,
            send_sem=send_sem.at[phase, d], recv_sem=recv_sem.at[phase, s],
            device_id={"seq": d}, device_id_type=MESH,
        )

    loads = [
        pltpu.make_async_copy(a, b, load_sem.at[i])
        for i, (a, b) in enumerate(((g_hbm, g), (x_hbm, x), (f_hbm, f), (k_hbm, k)))
    ]
    for c in loads:
        c.start()
    own_u = pltpu.make_async_copy(share(u_hbm, me), part(mu, me), own_sem.at[0])
    own_u.start()

    barrier = pltpu.get_barrier_semaphore()

    @pl.loop(1, n)
    def _(j):
        pl.semaphore_signal(
            barrier, inc=1, device_id={"seq": lax.rem(me + j, n)}, device_id_type=MESH
        )

    for j in range(1, dps):
        pl.semaphore_signal(
            barrier, inc=1, device_id={"dp": lax.rem(my_dp + j, dps)}, device_id_type=MESH
        )
    pl.semaphore_wait(barrier, n - 1 + dps - 1)

    @pl.loop(1, n)
    def _(j):
        d = lax.rem(me + j, n)
        copy_to(0, share(u_hbm, d), part(mu, me), d, me).start()

    for c in loads:
        c.wait()

    @pl.loop(0, lb)
    def _(i):
        sig = jax.nn.sigmoid(g[i].astype(F32))
        mixed[i] = (x[i].astype(F32) * sig).astype(BF)

    @pl.loop(0, w // 256)
    def _(j):
        cols = pl.ds(pl.multiple_of(j * 256, 256), 256)
        b = dot(mixed[...].reshape(lb * ch, w), f[cols, :], 1, 1)
        b = b.astype(BF).reshape(lb, ch, 256)
        blocks[:, :, cols] = b
        kern[:, :, cols] = (b.astype(F32) * k[:, :, cols].astype(F32)).astype(BF)

    def spread(r0, count, width):
        r = lax.broadcasted_iota(jnp.int32, (count, width), 0) + r0
        lo = lax.broadcasted_iota(jnp.int32, (count, width), 1) * CS
        return jnp.where((r >= lo) & (r < lo + CS), 1.0, 0.0)

    def same_channel():
        r = lax.broadcasted_iota(jnp.int32, (step_rows, rows), 0)
        c = lax.broadcasted_iota(jnp.int32, (step_rows, rows), 1)
        return (r & (CS - 1)) == (c & (CS - 1))

    def build(dst, dim):
        @pl.loop(0, steps)
        def _(j):
            r0 = pl.multiple_of(j * step_rows, step_rows)
            a = dot(spread(r0, step_rows, nb).astype(BF), s_ref[...], 1, dim).astype(BF)
            e = dot(a, spread(0, rows, nb).astype(BF), 1, 1)
            dst[pl.ds(r0, step_rows), :] = jnp.where(same_channel(), e, 0.0).astype(BF)

    def wait_in(phase, dst):
        @pl.loop(1, n)
        def _(j):
            s = lax.rem(me + j, n)
            copy_to(phase, part(dst, s), part(dst, s), s, s).wait_recv()

    def wait_back(phase, dst, share):
        @pl.loop(1, n)
        def _(j):
            s = lax.rem(me + j, n)
            copy_to(phase, share(dst, s), share(dst, s), s, s).wait_recv()

    def mix(phase, matrix, src, acc, dst, share, sem):
        width = src.shape[2]

        @pl.loop(0, steps)
        def _(j):
            at = lax.rem(lax.div(me, 4) + j, steps)
            r0 = pl.multiple_of(at * step_rows, step_rows)
            res = dot(matrix[pl.ds(r0, step_rows), :], src[...].reshape(rows, width), 1, 0)
            acc[pl.ds(at * 4 * lb, 4 * lb)] = res.astype(BF).reshape(4 * lb, CS, width)

            @pl.loop(0, 4)
            def _(i):
                d = at * 4 + i

                @pl.when(d != me)
                def _():
                    copy_to(phase, part(acc, d), share(dst, me), d, me).start()

        own = pltpu.make_async_copy(part(acc, me), share(dst, me), sem)
        own.start()
        return own

    def send_kern(half):
        own = pltpu.make_async_copy(
            share_of[half](kern, me), part(mk.at[half], me), own_sem.at[2 + half]
        )
        own.start()

        @pl.loop(1, n)
        def _(j):
            d = lax.rem(me + j, n)
            copy_to(2 + half, share_of[half](kern, d), part(mk.at[half], me), d, me).start()

        return own

    def mix_kern(half, own):
        own.wait()
        wait_in(2 + half, mk.at[half])
        return mix(
            4 + half, kron, mk.at[half], oac.at[half], om, share_of[half], own_sem.at[4 + half]
        )

    own_k0 = send_kern(0)
    build(kron_t, 1)
    build(kron, 0)
    own_u.wait()
    wait_in(0, mu)
    own_g = mix(1, kron_t, mu, gac, gm, share, own_sem.at[1])
    own_k1 = send_kern(1)

    own_g.wait()
    wait_back(1, gm, share)

    @pl.loop(0, lb)
    def _(i):
        mid = gm[i].astype(F32)
        gk[i] = (mid * blocks[i].astype(F32)).astype(BF)
        gb[i] = (mid * k[i].astype(F32)).astype(BF)

    gk_store = pltpu.make_async_copy(gk, gk_hbm, store_sem.at[0])
    gk_store.start()

    def place(owner):
        return sum(((owner >> b) & 1) * (w >> (b + 1)) for b in range(levels))

    for j in range(w // 256):
        cols = pl.ds(j * 256, 256)
        res = dot(gb[:, :, cols].reshape(lb * ch, 256), mixed[...].reshape(lb * ch, w), 0, 0)
        for i in range(256 // owned):
            gf[pl.ds(place(j * (256 // owned) + i), owned), :] = res[i * owned:(i + 1) * owned]

    base = 0
    offset = 0
    halves = []

    def half_start(level, base, offset):
        size = w >> (level + 1)
        bit = lax.rem(lax.div(me, 1 << level), 2)
        keep = pl.multiple_of(base + bit * size, owned)
        give = pl.multiple_of(base + (1 - bit) * size, owned)

        @pl.loop(0, size // owned)
        def _(i):
            to = pl.multiple_of(offset + i * owned, owned)
            rs_send[pl.ds(to, owned), :] = gf[pl.ds(give + i * owned, owned), :].astype(BF)

        copy = pltpu.make_async_remote_copy(
            src_ref=rs_send.at[pl.ds(offset, size)], dst_ref=rs_recv.at[pl.ds(offset, size)],
            send_sem=rs_ssem.at[level], recv_sem=rs_rsem.at[level],
            device_id={"seq": me + (1 - 2 * bit) * (1 << level)}, device_id_type=MESH,
        )
        copy.start()
        halves.append(copy)
        return keep, offset + size

    def half_end(level, keep, offset):
        size = w >> (level + 1)
        halves[level].wait_recv()

        @pl.loop(0, size // owned)
        def _(i):
            at = pl.ds(pl.multiple_of(keep + i * owned, owned), owned)
            come = pl.ds(pl.multiple_of(offset - size + i * owned, owned), owned)
            gf[at, :] = gf[at, :] + rs_recv[come, :].astype(F32)

    base, offset = half_start(0, base, offset)
    own_o0 = mix_kern(0, own_k0)

    @pl.loop(0, lb)
    def _(i):
        gmx = dot(gb[i], f[...], 1, 0)
        sig = jax.nn.sigmoid(g[i].astype(F32))
        gi[i] = (gmx * sig).astype(BF)
        gg[i] = (gmx * x[i].astype(F32) * sig * (1.0 - sig)).astype(BF)

    gi_store = pltpu.make_async_copy(gi, gi_hbm, store_sem.at[1])
    gi_store.start()
    gg_store = pltpu.make_async_copy(gg, gg_hbm, store_sem.at[2])
    gg_store.start()

    half_end(0, base, offset)
    base, offset = half_start(1, base, offset)

    own_o1 = mix_kern(1, own_k1)

    half_end(1, base, offset)
    base, offset = half_start(2, base, offset)

    lanes = g2s.shape[2]
    g2s[...] = jnp.zeros_like(g2s)
    for j in range(steps):
        part_u = mu[pl.ds(j * 4 * lb, 4 * lb)].reshape(step_rows, pw)
        h = dot(part_u[:, :hw], mk[0].reshape(rows, hw), 1, 1)
        h = h + dot(part_u[:, hw:], mk[1].reshape(rows, hw), 1, 1)
        h = jnp.where(same_channel(), h, 0.0).reshape(4 * lb, CS, rows).sum(axis=1)
        h = dot(h, spread(0, rows, lanes), 1, 0, precision=lax.Precision.HIGHEST)
        for i in range(4):
            g2s[j * 4 + i, 0:lb, :] = h[i * lb:(i + 1) * lb]

    def g2_copy(d, s):
        return pltpu.make_async_remote_copy(
            src_ref=g2s.at[d], dst_ref=g2r.at[s],
            send_sem=g2_ssem.at[d], recv_sem=g2_rsem.at[s],
            device_id={"seq": d}, device_id_type=MESH,
        )

    @pl.loop(1, n)
    def _(j):
        d = lax.rem(me + j, n)
        g2_copy(d, me).start()

    g2r[pl.ds(me, 1)] = g2s[pl.ds(me, 1)]

    for level in range(2, levels):
        half_end(level, base, offset)
        if level + 1 < levels:
            base, offset = half_start(level + 1, base, offset)

    @pl.loop(1, n)
    def _(j):
        s = lax.rem(me + j, n)
        g2_copy(s, s).wait_recv()

    dpbuf[pl.ds(my_dp, 1)] = gf[pl.ds(base, owned), :].astype(BF)[None]
    g2dp[pl.ds(my_dp, 1)] = jnp.sum(g2r[...], axis=0, keepdims=True)

    def dp_copies(d, s):
        return [
            pltpu.make_async_remote_copy(
                src_ref=buf.at[s], dst_ref=buf.at[s],
                send_sem=dp_ssem.at[i, d], recv_sem=dp_rsem.at[i, s],
                device_id={"dp": d}, device_id_type=MESH,
            )
            for i, buf in enumerate((dpbuf, g2dp))
        ]

    for j in range(1, dps):
        for c in dp_copies(lax.rem(my_dp + j, dps), my_dp):
            c.start()
    for j in range(1, dps):
        s = lax.rem(my_dp + j, dps)
        for c in dp_copies(s, s):
            c.wait_recv()
    first = dpbuf[0].astype(F32)
    second = g2dp[0]
    for i in range(1, dps):
        first = first + dpbuf[i].astype(F32)
        second = second + g2dp[i]
    gf_ref[...] = first * (1.0 / math.sqrt(nb * ch * dps))
    gs_ref[...] = second[0:lb, 0:nb] * (1.0 / math.sqrt(ch * dps * w))

    own_o0.wait()
    own_o1.wait()
    wait_back(4, om, share_of[0])
    wait_back(5, om, share_of[1])
    out_store = pltpu.make_async_copy(om, out_hbm, store_sem.at[3])
    out_store.start()

    @pl.loop(1, n)
    def _(j):
        d = lax.rem(me + j, n)
        copy_to(0, share(u_hbm, d), part(mu, me), d, me).wait_send()
        copy_to(1, part(gac, d), share(gm, me), d, me).wait_send()
        for i in range(2):
            copy_to(2 + i, share_of[i](kern, d), part(mk.at[i], me), d, me).wait_send()
            copy_to(4 + i, part(oac.at[i], d), share_of[i](om, me), d, me).wait_send()
        g2_copy(d, me).wait_send()

    for c in halves:
        c.wait_send()
    for j in range(1, dps):
        for c in dp_copies(lax.rem(my_dp + j, dps), my_dp):
            c.wait_send()
    gk_store.wait()
    gi_store.wait()
    gg_store.wait()
    out_store.wait()


def hand_over(*refs):
    sems = refs[12]
    copies = []
    for i, (src, dst) in enumerate(zip(refs[:6], refs[6:12])):
        if len(src.shape) == 3:
            for j in range(src.shape[0]):
                copies.append(pltpu.make_async_copy(src.at[j], dst.at[j], sems.at[i, j]))
        else:
            copies.append(pltpu.make_async_copy(src, dst, sems.at[i, 0]))
    for c in copies:
        c.start()
    for c in copies:
        c.wait()


def on_device(n, dps, inputs, gates, kernel, first_factor, second_factor, upstream):
    lb, ch, w = inputs.shape
    nb = second_factor.shape[0]
    pw = w // (n // (ch // CS))
    owned = w // n
    levels = n.bit_length() - 1
    lanes = max(nb, 128)
    act = jax.ShapeDtypeStruct((lb, ch, w), BF)
    a_act = pltpu.VMEM((lb, ch, w), BF)
    a_mov = pltpu.VMEM((nb, CS, pw), BF)
    a_half = pltpu.VMEM((2, nb, CS, pw // 2), BF)
    hbm = pl.BlockSpec(memory_space=pl.ANY)
    vmem = pl.BlockSpec(memory_space=pltpu.VMEM)
    sem = pltpu.SemaphoreType.DMA
    flops = 6 * lb * ch * w * w
    results = pl.pallas_call(
        functools.partial(layer_kernel, n, dps, lb, ch, w, nb),
        out_shape=(
            act, act, act, act,
            jax.ShapeDtypeStruct((owned, w), F32),
            jax.ShapeDtypeStruct((lb, nb), F32),
        ),
        in_specs=[hbm, hbm, hbm, hbm, vmem, hbm],
        out_specs=(hbm, hbm, hbm, hbm, vmem, vmem),
        scratch_shapes=[
            a_act, a_act, a_act, pltpu.VMEM((w, w), BF),
            a_act, a_act, a_act,
            a_mov, a_half, a_mov, a_half,
            a_act, a_act, a_act, a_act, a_act, a_act,
            pltpu.VMEM((nb * CS, nb * CS), BF), pltpu.VMEM((nb * CS, nb * CS), BF),
            pltpu.VMEM((w, w), F32),
            pltpu.VMEM((w, w), BF), pltpu.VMEM((w, w), BF),
            pltpu.VMEM((dps, owned, w), BF),
            pltpu.VMEM((n, 8, lanes), F32), pltpu.VMEM((n, 8, lanes), F32),
            pltpu.VMEM((dps, 8, lanes), F32),
            sem((4,)), sem((6,)), sem((4,)), sem((6, n)), sem((6, n)),
            sem((levels,)), sem((levels,)), sem((n,)), sem((n,)), sem((2, dps)), sem((2, dps)),
        ],
        compiler_params=pltpu.CompilerParams(
            collective_id=0, has_side_effects=True, vmem_limit_bytes=58 * 1024 * 1024
        ),
        cost_estimate=pl.CostEstimate(flops=flops, bytes_accessed=10 << 20, transcendentals=0),
    )(inputs, gates, kernel, first_factor, second_factor, upstream)
    return pl.pallas_call(
        hand_over,
        out_shape=tuple(jax.ShapeDtypeStruct(r.shape, r.dtype) for r in results),
        in_specs=[hbm] * 6,
        out_specs=(hbm,) * 6,
        scratch_shapes=[sem((6, lb))],
        compiler_params=pltpu.CompilerParams(vmem_limit_bytes=60 * 1024 * 1024),
        cost_estimate=pl.CostEstimate(flops=0, bytes_accessed=8 << 20, transcendentals=0),
    )(*results)


def solution(mesh):
    cut = P("seq", "dp", None)
    return jax.shard_map(
        functools.partial(on_device, mesh.shape["seq"], mesh.shape["dp"]),
        mesh=mesh,
        in_specs=(cut, cut, cut, P(), P(), cut),
        out_specs=(cut, cut, cut, cut, P("seq", None), P("seq", None)),
        check_vma=False,
    )
```

```python
import functools
import math

import jax
import jax.numpy as jnp
from jax import lax
from jax.experimental import pallas as pl
from jax.experimental.pallas import tpu as pltpu
from jax.sharding import PartitionSpec as P

MESH = pl.DeviceIdType.MESH
BF = jnp.bfloat16
F32 = jnp.float32
CS = 16


def dot(a, b, ca, cb, **kw):
    return lax.dot_general(a, b, (((ca,), (cb,)), ((), ())), preferred_element_type=F32, **kw)


def layer_kernel(
    n, dps, lb, ch, w, nb,
    x_hbm, g_hbm, k_hbm, f_hbm, s_ref, u_hbm,
    out_hbm, gi_hbm, gg_hbm, gk_hbm, gf_ref, gs_ref,
    x, g, k, f, mixed, blocks, kern, mu, mk, gac, oac, gm, om, gb, gi, gg, gk,
    kron, kron_t, gf, rs_send, rs_recv, dpbuf, g2s, g2r, g2dp,
    load_sem, own_sem, store_sem, send_sem, recv_sem, rs_ssem, rs_rsem,
    g2_ssem, g2_rsem, dp_ssem, dp_rsem,
):
    me = lax.axis_index("seq")
    my_dp = lax.axis_index("dp")
    pg = n // (ch // CS)
    pw = w // pg
    rows = nb * CS
    step_rows = 4 * lb * CS
    steps = n // 4
    owned = w // n
    levels = n.bit_length() - 1

    def share(ref, d):
        c0 = pl.multiple_of(lax.div(d, pg) * CS, CS)
        p0 = pl.multiple_of(lax.rem(d, pg) * pw, pw)
        return ref.at[:, pl.ds(c0, CS), pl.ds(p0, pw)]

    def part(ref, d):
        return ref.at[pl.ds(d * lb, lb)]

    def copy_to(phase, src, dst, d, s):
        return pltpu.make_async_remote_copy(
            src_ref=src, dst_ref=dst,
            send_sem=send_sem.at[phase, d], recv_sem=recv_sem.at[phase, s],
            device_id={"seq": d}, device_id_type=MESH,
        )

    loads = [
        pltpu.make_async_copy(a, b, load_sem.at[i])
        for i, (a, b) in enumerate(((g_hbm, g), (x_hbm, x), (f_hbm, f), (k_hbm, k)))
    ]
    for c in loads:
        c.start()
    own_u = pltpu.make_async_copy(share(u_hbm, me), part(mu, me), own_sem.at[0])
    own_u.start()

    barrier = pltpu.get_barrier_semaphore()

    @pl.loop(1, n)
    def _(j):
        pl.semaphore_signal(
            barrier, inc=1, device_id={"seq": lax.rem(me + j, n)}, device_id_type=MESH
        )

    for j in range(1, dps):
        pl.semaphore_signal(
            barrier, inc=1, device_id={"dp": lax.rem(my_dp + j, dps)}, device_id_type=MESH
        )
    pl.semaphore_wait(barrier, n - 1 + dps - 1)

    @pl.loop(1, n)
    def _(j):
        d = lax.rem(me + j, n)
        copy_to(0, share(u_hbm, d), part(mu, me), d, me).start()

    for c in loads:
        c.wait()

    @pl.loop(0, lb)
    def _(i):
        sig = jax.nn.sigmoid(g[i].astype(F32))
        mixed[i] = (x[i].astype(F32) * sig).astype(BF)

    @pl.loop(0, w // 256)
    def _(j):
        cols = pl.ds(pl.multiple_of(j * 256, 256), 256)
        b = dot(mixed[...].reshape(lb * ch, w), f[cols, :], 1, 1)
        b = b.astype(BF).reshape(lb, ch, 256)
        blocks[:, :, cols] = b
        kern[:, :, cols] = (b.astype(F32) * k[:, :, cols].astype(F32)).astype(BF)

    def spread(r0, count, width):
        r = lax.broadcasted_iota(jnp.int32, (count, width), 0) + r0
        lo = lax.broadcasted_iota(jnp.int32, (count, width), 1) * CS
        return jnp.where((r >= lo) & (r < lo + CS), 1.0, 0.0)

    def same_channel():
        r = lax.broadcasted_iota(jnp.int32, (step_rows, rows), 0)
        c = lax.broadcasted_iota(jnp.int32, (step_rows, rows), 1)
        return (r & (CS - 1)) == (c & (CS - 1))

    def build(dst, dim):
        @pl.loop(0, steps)
        def _(j):
            r0 = pl.multiple_of(j * step_rows, step_rows)
            a = dot(spread(r0, step_rows, nb).astype(BF), s_ref[...], 1, dim).astype(BF)
            e = dot(a, spread(0, rows, nb).astype(BF), 1, 1)
            dst[pl.ds(r0, step_rows), :] = jnp.where(same_channel(), e, 0.0).astype(BF)

    build(kron_t, 1)
    build(kron, 0)

    def wait_in(phase, dst):
        @pl.loop(1, n)
        def _(j):
            s = lax.rem(me + j, n)
            copy_to(phase, part(dst, s), part(dst, s), s, s).wait_recv()

    def wait_back(phase, dst):
        @pl.loop(1, n)
        def _(j):
            s = lax.rem(me + j, n)
            copy_to(phase, share(dst, s), share(dst, s), s, s).wait_recv()

    def mix(phase, matrix, src, acc, dst, sem):
        @pl.loop(0, steps)
        def _(j):
            at = lax.rem(lax.div(me, 4) + j, steps)
            r0 = pl.multiple_of(at * step_rows, step_rows)
            res = dot(matrix[pl.ds(r0, step_rows), :], src[...].reshape(rows, pw), 1, 0)
            acc[pl.ds(at * 4 * lb, 4 * lb)] = res.astype(BF).reshape(4 * lb, CS, pw)

            @pl.loop(0, 4)
            def _(i):
                d = at * 4 + i

                @pl.when(d != me)
                def _():
                    copy_to(phase, part(acc, d), share(dst, me), d, me).start()

        own = pltpu.make_async_copy(part(acc, me), share(dst, me), sem)
        own.start()
        return own

    own_u.wait()
    wait_in(0, mu)
    own_g = mix(1, kron_t, mu, gac, gm, own_sem.at[1])

    own_k = pltpu.make_async_copy(share(kern, me), part(mk, me), own_sem.at[2])
    own_k.start()

    @pl.loop(1, n)
    def _(j):
        d = lax.rem(me + j, n)
        copy_to(2, share(kern, d), part(mk, me), d, me).start()

    own_g.wait()
    wait_back(1, gm)

    @pl.loop(0, lb)
    def _(i):
        mid = gm[i].astype(F32)
        gk[i] = (mid * blocks[i].astype(F32)).astype(BF)
        gb[i] = (mid * k[i].astype(F32)).astype(BF)

    gk_store = pltpu.make_async_copy(gk, gk_hbm, store_sem.at[0])
    gk_store.start()

    def place(owner):
        return sum(((owner >> b) & 1) * (w >> (b + 1)) for b in range(levels))

    for j in range(w // 256):
        cols = pl.ds(j * 256, 256)
        res = dot(gb[:, :, cols].reshape(lb * ch, 256), mixed[...].reshape(lb * ch, w), 0, 0)
        for i in range(256 // owned):
            gf[pl.ds(place(j * (256 // owned) + i), owned), :] = res[i * owned:(i + 1) * owned]

    base = 0
    offset = 0
    halves = []

    def half_start(level, base, offset):
        size = w >> (level + 1)
        bit = lax.rem(lax.div(me, 1 << level), 2)
        keep = pl.multiple_of(base + bit * size, owned)
        give = pl.multiple_of(base + (1 - bit) * size, owned)

        @pl.loop(0, size // owned)
        def _(i):
            to = pl.multiple_of(offset + i * owned, owned)
            rs_send[pl.ds(to, owned), :] = gf[pl.ds(give + i * owned, owned), :].astype(BF)

        copy = pltpu.make_async_remote_copy(
            src_ref=rs_send.at[pl.ds(offset, size)], dst_ref=rs_recv.at[pl.ds(offset, size)],
            send_sem=rs_ssem.at[level], recv_sem=rs_rsem.at[level],
            device_id={"seq": me + (1 - 2 * bit) * (1 << level)}, device_id_type=MESH,
        )
        copy.start()
        halves.append(copy)
        return keep, offset + size

    def half_end(level, keep, offset):
        size = w >> (level + 1)
        halves[level].wait_recv()

        @pl.loop(0, size // owned)
        def _(i):
            at = pl.ds(pl.multiple_of(keep + i * owned, owned), owned)
            come = pl.ds(pl.multiple_of(offset - size + i * owned, owned), owned)
            gf[at, :] = gf[at, :] + rs_recv[come, :].astype(F32)

    base, offset = half_start(0, base, offset)

    @pl.loop(0, lb)
    def _(i):
        gmx = dot(gb[i], f[...], 1, 0)
        sig = jax.nn.sigmoid(g[i].astype(F32))
        gi[i] = (gmx * sig).astype(BF)
        gg[i] = (gmx * x[i].astype(F32) * sig * (1.0 - sig)).astype(BF)

    gi_store = pltpu.make_async_copy(gi, gi_hbm, store_sem.at[1])
    gi_store.start()
    gg_store = pltpu.make_async_copy(gg, gg_hbm, store_sem.at[2])
    gg_store.start()

    half_end(0, base, offset)
    base, offset = half_start(1, base, offset)

    own_k.wait()
    wait_in(2, mk)
    own_o = mix(3, kron, mk, oac, om, own_sem.at[3])

    half_end(1, base, offset)
    base, offset = half_start(2, base, offset)

    lanes = g2s.shape[2]
    g2s[...] = jnp.zeros_like(g2s)
    for j in range(steps):
        part_u = mu[pl.ds(j * 4 * lb, 4 * lb)].reshape(step_rows, pw)
        h = dot(part_u, mk[...].reshape(rows, pw), 1, 1)
        h = jnp.where(same_channel(), h, 0.0).reshape(4 * lb, CS, rows).sum(axis=1)
        h = dot(h, spread(0, rows, lanes), 1, 0, precision=lax.Precision.HIGHEST)
        for i in range(4):
            g2s[j * 4 + i, 0:lb, :] = h[i * lb:(i + 1) * lb]

    def g2_copy(d, s):
        return pltpu.make_async_remote_copy(
            src_ref=g2s.at[d], dst_ref=g2r.at[s],
            send_sem=g2_ssem.at[d], recv_sem=g2_rsem.at[s],
            device_id={"seq": d}, device_id_type=MESH,
        )

    @pl.loop(1, n)
    def _(j):
        d = lax.rem(me + j, n)
        g2_copy(d, me).start()

    g2r[pl.ds(me, 1)] = g2s[pl.ds(me, 1)]

    for level in range(2, levels):
        half_end(level, base, offset)
        if level + 1 < levels:
            base, offset = half_start(level + 1, base, offset)

    @pl.loop(1, n)
    def _(j):
        s = lax.rem(me + j, n)
        g2_copy(s, s).wait_recv()

    dpbuf[pl.ds(my_dp, 1)] = gf[pl.ds(base, owned), :].astype(BF)[None]
    g2dp[pl.ds(my_dp, 1)] = jnp.sum(g2r[...], axis=0, keepdims=True)

    def dp_copies(d, s):
        return [
            pltpu.make_async_remote_copy(
                src_ref=buf.at[s], dst_ref=buf.at[s],
                send_sem=dp_ssem.at[i, d], recv_sem=dp_rsem.at[i, s],
                device_id={"dp": d}, device_id_type=MESH,
            )
            for i, buf in enumerate((dpbuf, g2dp))
        ]

    for j in range(1, dps):
        for c in dp_copies(lax.rem(my_dp + j, dps), my_dp):
            c.start()
    for j in range(1, dps):
        s = lax.rem(my_dp + j, dps)
        for c in dp_copies(s, s):
            c.wait_recv()
    first = dpbuf[0].astype(F32)
    second = g2dp[0]
    for i in range(1, dps):
        first = first + dpbuf[i].astype(F32)
        second = second + g2dp[i]
    gf_ref[...] = first * (1.0 / math.sqrt(nb * ch * dps))
    gs_ref[...] = second[0:lb, 0:nb] * (1.0 / math.sqrt(ch * dps * w))

    own_o.wait()
    wait_back(3, om)
    out_store = pltpu.make_async_copy(om, out_hbm, store_sem.at[3])
    out_store.start()

    @pl.loop(1, n)
    def _(j):
        d = lax.rem(me + j, n)
        copy_to(0, share(u_hbm, d), part(mu, me), d, me).wait_send()
        copy_to(1, part(gac, d), share(gm, me), d, me).wait_send()
        copy_to(2, share(kern, d), part(mk, me), d, me).wait_send()
        copy_to(3, part(oac, d), share(om, me), d, me).wait_send()
        g2_copy(d, me).wait_send()

    for c in halves:
        c.wait_send()
    for j in range(1, dps):
        for c in dp_copies(lax.rem(my_dp + j, dps), my_dp):
            c.wait_send()
    gk_store.wait()
    gi_store.wait()
    gg_store.wait()
    out_store.wait()


def hand_over(*refs):
    for src, dst in zip(refs[:6], refs[6:]):
        dst[...] = src[...]


def on_device(n, dps, inputs, gates, kernel, first_factor, second_factor, upstream):
    lb, ch, w = inputs.shape
    nb = second_factor.shape[0]
    pw = w // (n // (ch // CS))
    owned = w // n
    levels = n.bit_length() - 1
    lanes = max(nb, 128)
    act = jax.ShapeDtypeStruct((lb, ch, w), BF)
    a_act = pltpu.VMEM((lb, ch, w), BF)
    a_mov = pltpu.VMEM((nb, CS, pw), BF)
    hbm = pl.BlockSpec(memory_space=pl.ANY)
    vmem = pl.BlockSpec(memory_space=pltpu.VMEM)
    sem = pltpu.SemaphoreType.DMA
    flops = 6 * lb * ch * w * w
    results = pl.pallas_call(
        functools.partial(layer_kernel, n, dps, lb, ch, w, nb),
        out_shape=(
            act, act, act, act,
            jax.ShapeDtypeStruct((owned, w), F32),
            jax.ShapeDtypeStruct((lb, nb), F32),
        ),
        in_specs=[hbm, hbm, hbm, hbm, vmem, hbm],
        out_specs=(hbm, hbm, hbm, hbm, vmem, vmem),
        scratch_shapes=[
            a_act, a_act, a_act, pltpu.VMEM((w, w), BF),
            a_act, a_act, a_act,
            a_mov, a_mov, a_mov, a_mov,
            a_act, a_act, a_act, a_act, a_act, a_act,
            pltpu.VMEM((nb * CS, nb * CS), BF), pltpu.VMEM((nb * CS, nb * CS), BF),
            pltpu.VMEM((w, w), F32),
            pltpu.VMEM((w, w), BF), pltpu.VMEM((w, w), BF),
            pltpu.VMEM((dps, owned, w), BF),
            pltpu.VMEM((n, 8, lanes), F32), pltpu.VMEM((n, 8, lanes), F32),
            pltpu.VMEM((dps, 8, lanes), F32),
            sem((4,)), sem((4,)), sem((4,)), sem((4, n)), sem((4, n)),
            sem((levels,)), sem((levels,)), sem((n,)), sem((n,)), sem((2, dps)), sem((2, dps)),
        ],
        compiler_params=pltpu.CompilerParams(
            collective_id=0, has_side_effects=True, vmem_limit_bytes=58 * 1024 * 1024
        ),
        cost_estimate=pl.CostEstimate(flops=flops, bytes_accessed=10 << 20, transcendentals=0),
    )(inputs, gates, kernel, first_factor, second_factor, upstream)
    block = pl.BlockSpec((1, ch, w), lambda i: (i, 0, 0))
    specs = [block] * 4 + [pl.BlockSpec(r.shape, lambda i: (0, 0)) for r in results[4:]]
    return pl.pallas_call(
        hand_over,
        grid=(lb,),
        out_shape=tuple(jax.ShapeDtypeStruct(r.shape, r.dtype) for r in results),
        in_specs=specs,
        out_specs=tuple(specs),
        compiler_params=pltpu.CompilerParams(vmem_limit_bytes=60 * 1024 * 1024),
        cost_estimate=pl.CostEstimate(flops=0, bytes_accessed=8 << 20, transcendentals=0),
    )(*results)


def solution(mesh):
    cut = P("seq", "dp", None)
    return jax.shard_map(
        functools.partial(on_device, mesh.shape["seq"], mesh.shape["dp"]),
        mesh=mesh,
        in_specs=(cut, cut, cut, P(), P(), cut),
        out_specs=(cut, cut, cut, cut, P("seq", None), P("seq", None)),
        check_vma=False,
    )
```

```python
import functools
import math

import jax
import jax.numpy as jnp
from jax import lax
from jax.experimental import pallas as pl
from jax.experimental.pallas import tpu as pltpu
from jax.sharding import PartitionSpec as P

MESH = pl.DeviceIdType.MESH
BF = jnp.bfloat16
F32 = jnp.float32
CS = 16


def dot(a, b, ca, cb, **kw):
    return lax.dot_general(a, b, (((ca,), (cb,)), ((), ())), preferred_element_type=F32, **kw)


def layer_kernel(
    n, dps, lb, ch, w, nb,
    x_hbm, g_hbm, k_hbm, f_hbm, s_ref, u_hbm,
    out_hbm, gi_hbm, gg_hbm, gk_hbm, gf_ref, gs_ref,
    x, g, k, f, mixed, blocks, kern, mu, mk, gac, oac, gm, om, gb, gi, gg, gk,
    kron, kron_t, gf, rs_send, rs_recv, dpbuf, g2s, g2r, g2dp,
    load_sem, own_sem, store_sem, send_sem, recv_sem, rs_ssem, rs_rsem,
    g2_ssem, g2_rsem, dp_ssem, dp_rsem,
):
    me = lax.axis_index("seq")
    my_dp = lax.axis_index("dp")
    pg = n // (ch // CS)
    pw = w // pg
    rows = nb * CS
    step_rows = 4 * lb * CS
    steps = n // 4
    owned = w // n
    levels = n.bit_length() - 1

    def share(ref, d):
        c0 = pl.multiple_of(lax.div(d, pg) * CS, CS)
        p0 = pl.multiple_of(lax.rem(d, pg) * pw, pw)
        return ref.at[:, pl.ds(c0, CS), pl.ds(p0, pw)]

    def part(ref, d):
        return ref.at[pl.ds(d * lb, lb)]

    def copy_to(phase, src, dst, d, s):
        return pltpu.make_async_remote_copy(
            src_ref=src, dst_ref=dst,
            send_sem=send_sem.at[phase, d], recv_sem=recv_sem.at[phase, s],
            device_id={"seq": d}, device_id_type=MESH,
        )

    loads = [
        pltpu.make_async_copy(a, b, load_sem.at[i])
        for i, (a, b) in enumerate(((g_hbm, g), (x_hbm, x), (f_hbm, f), (k_hbm, k)))
    ]
    for c in loads:
        c.start()
    own_u = pltpu.make_async_copy(share(u_hbm, me), part(mu, me), own_sem.at[0])
    own_u.start()

    barrier = pltpu.get_barrier_semaphore()

    @pl.loop(1, n)
    def _(j):
        pl.semaphore_signal(
            barrier, inc=1, device_id={"seq": lax.rem(me + j, n)}, device_id_type=MESH
        )

    for j in range(1, dps):
        pl.semaphore_signal(
            barrier, inc=1, device_id={"dp": lax.rem(my_dp + j, dps)}, device_id_type=MESH
        )
    pl.semaphore_wait(barrier, n - 1 + dps - 1)

    @pl.loop(1, n)
    def _(j):
        d = lax.rem(me + j, n)
        copy_to(0, share(u_hbm, d), part(mu, me), d, me).start()

    for c in loads:
        c.wait()

    @pl.loop(0, lb)
    def _(i):
        sig = jax.nn.sigmoid(g[i].astype(F32))
        mixed[i] = (x[i].astype(F32) * sig).astype(BF)

    @pl.loop(0, w // 256)
    def _(j):
        cols = pl.ds(pl.multiple_of(j * 256, 256), 256)
        b = dot(mixed[...].reshape(lb * ch, w), f[cols, :], 1, 1)
        b = b.astype(BF).reshape(lb, ch, 256)
        blocks[:, :, cols] = b
        kern[:, :, cols] = (b.astype(F32) * k[:, :, cols].astype(F32)).astype(BF)

    def spread(r0, count, width):
        r = lax.broadcasted_iota(jnp.int32, (count, width), 0) + r0
        lo = lax.broadcasted_iota(jnp.int32, (count, width), 1) * CS
        return jnp.where((r >= lo) & (r < lo + CS), 1.0, 0.0)

    def same_channel():
        r = lax.broadcasted_iota(jnp.int32, (step_rows, rows), 0)
        c = lax.broadcasted_iota(jnp.int32, (step_rows, rows), 1)
        return (r & (CS - 1)) == (c & (CS - 1))

    def build(dst, dim):
        @pl.loop(0, steps)
        def _(j):
            r0 = pl.multiple_of(j * step_rows, step_rows)
            a = dot(spread(r0, step_rows, nb).astype(BF), s_ref[...], 1, dim).astype(BF)
            e = dot(a, spread(0, rows, nb).astype(BF), 1, 1)
            dst[pl.ds(r0, step_rows), :] = jnp.where(same_channel(), e, 0.0).astype(BF)

    build(kron_t, 1)
    build(kron, 0)

    def wait_in(phase, dst):
        @pl.loop(1, n)
        def _(j):
            s = lax.rem(me + j, n)
            copy_to(phase, part(dst, s), part(dst, s), s, s).wait_recv()

    def wait_back(phase, dst):
        @pl.loop(1, n)
        def _(j):
            s = lax.rem(me + j, n)
            copy_to(phase, share(dst, s), share(dst, s), s, s).wait_recv()

    def mix(phase, matrix, src, acc, dst, sem):
        @pl.loop(0, steps)
        def _(j):
            at = lax.rem(lax.div(me, 4) + j, steps)
            r0 = pl.multiple_of(at * step_rows, step_rows)
            res = dot(matrix[pl.ds(r0, step_rows), :], src[...].reshape(rows, pw), 1, 0)
            acc[pl.ds(at * 4 * lb, 4 * lb)] = res.astype(BF).reshape(4 * lb, CS, pw)

            @pl.loop(0, 4)
            def _(i):
                d = at * 4 + i

                @pl.when(d != me)
                def _():
                    copy_to(phase, part(acc, d), share(dst, me), d, me).start()

        own = pltpu.make_async_copy(part(acc, me), share(dst, me), sem)
        own.start()
        return own

    own_u.wait()
    wait_in(0, mu)
    own_g = mix(1, kron_t, mu, gac, gm, own_sem.at[1])

    own_k = pltpu.make_async_copy(share(kern, me), part(mk, me), own_sem.at[2])
    own_k.start()

    @pl.loop(1, n)
    def _(j):
        d = lax.rem(me + j, n)
        copy_to(2, share(kern, d), part(mk, me), d, me).start()

    own_g.wait()
    wait_back(1, gm)

    @pl.loop(0, lb)
    def _(i):
        mid = gm[i].astype(F32)
        gk[i] = (mid * blocks[i].astype(F32)).astype(BF)
        gb[i] = (mid * k[i].astype(F32)).astype(BF)

    gk_store = pltpu.make_async_copy(gk, gk_hbm, store_sem.at[0])
    gk_store.start()

    def place(owner):
        return sum(((owner >> b) & 1) * (w >> (b + 1)) for b in range(levels))

    for j in range(w // 256):
        cols = pl.ds(j * 256, 256)
        res = dot(gb[:, :, cols].reshape(lb * ch, 256), mixed[...].reshape(lb * ch, w), 0, 0)
        for i in range(256 // owned):
            gf[pl.ds(place(j * (256 // owned) + i), owned), :] = res[i * owned:(i + 1) * owned]

    base = 0
    offset = 0
    halves = []

    def half_start(level, base, offset):
        size = w >> (level + 1)
        bit = lax.rem(lax.div(me, 1 << level), 2)
        keep = pl.multiple_of(base + bit * size, owned)
        give = pl.multiple_of(base + (1 - bit) * size, owned)

        @pl.loop(0, size // owned)
        def _(i):
            to = pl.multiple_of(offset + i * owned, owned)
            rs_send[pl.ds(to, owned), :] = gf[pl.ds(give + i * owned, owned), :].astype(BF)

        copy = pltpu.make_async_remote_copy(
            src_ref=rs_send.at[pl.ds(offset, size)], dst_ref=rs_recv.at[pl.ds(offset, size)],
            send_sem=rs_ssem.at[level], recv_sem=rs_rsem.at[level],
            device_id={"seq": me + (1 - 2 * bit) * (1 << level)}, device_id_type=MESH,
        )
        copy.start()
        halves.append(copy)
        return keep, offset + size

    def half_end(level, keep, offset):
        size = w >> (level + 1)
        halves[level].wait_recv()

        @pl.loop(0, size // owned)
        def _(i):
            at = pl.ds(pl.multiple_of(keep + i * owned, owned), owned)
            come = pl.ds(pl.multiple_of(offset - size + i * owned, owned), owned)
            gf[at, :] = gf[at, :] + rs_recv[come, :].astype(F32)

    base, offset = half_start(0, base, offset)

    @pl.loop(0, lb)
    def _(i):
        gmx = dot(gb[i], f[...], 1, 0)
        sig = jax.nn.sigmoid(g[i].astype(F32))
        gi[i] = (gmx * sig).astype(BF)
        gg[i] = (gmx * x[i].astype(F32) * sig * (1.0 - sig)).astype(BF)

    gi_store = pltpu.make_async_copy(gi, gi_hbm, store_sem.at[1])
    gi_store.start()
    gg_store = pltpu.make_async_copy(gg, gg_hbm, store_sem.at[2])
    gg_store.start()

    half_end(0, base, offset)
    base, offset = half_start(1, base, offset)

    half_end(1, base, offset)
    base, offset = half_start(2, base, offset)

    own_k.wait()
    wait_in(2, mk)
    own_o = mix(3, kron, mk, oac, om, own_sem.at[3])

    lanes = g2s.shape[2]
    g2s[...] = jnp.zeros_like(g2s)
    for j in range(steps):
        part_u = mu[pl.ds(j * 4 * lb, 4 * lb)].reshape(step_rows, pw)
        h = dot(part_u, mk[...].reshape(rows, pw), 1, 1)
        h = jnp.where(same_channel(), h, 0.0).reshape(4 * lb, CS, rows).sum(axis=1)
        h = dot(h, spread(0, rows, lanes), 1, 0, precision=lax.Precision.HIGHEST)
        for i in range(4):
            g2s[j * 4 + i, 0:lb, :] = h[i * lb:(i + 1) * lb]

    def g2_copy(d, s):
        return pltpu.make_async_remote_copy(
            src_ref=g2s.at[d], dst_ref=g2r.at[s],
            send_sem=g2_ssem.at[d], recv_sem=g2_rsem.at[s],
            device_id={"seq": d}, device_id_type=MESH,
        )

    @pl.loop(1, n)
    def _(j):
        d = lax.rem(me + j, n)
        g2_copy(d, me).start()

    g2r[pl.ds(me, 1)] = g2s[pl.ds(me, 1)]

    for level in range(2, levels):
        half_end(level, base, offset)
        if level + 1 < levels:
            base, offset = half_start(level + 1, base, offset)

    @pl.loop(1, n)
    def _(j):
        s = lax.rem(me + j, n)
        g2_copy(s, s).wait_recv()

    dpbuf[pl.ds(my_dp, 1)] = gf[pl.ds(base, owned), :].astype(BF)[None]
    g2dp[pl.ds(my_dp, 1)] = jnp.sum(g2r[...], axis=0, keepdims=True)

    def dp_copies(d, s):
        return [
            pltpu.make_async_remote_copy(
                src_ref=buf.at[s], dst_ref=buf.at[s],
                send_sem=dp_ssem.at[i, d], recv_sem=dp_rsem.at[i, s],
                device_id={"dp": d}, device_id_type=MESH,
            )
            for i, buf in enumerate((dpbuf, g2dp))
        ]

    for j in range(1, dps):
        for c in dp_copies(lax.rem(my_dp + j, dps), my_dp):
            c.start()
    for j in range(1, dps):
        s = lax.rem(my_dp + j, dps)
        for c in dp_copies(s, s):
            c.wait_recv()
    first = dpbuf[0].astype(F32)
    second = g2dp[0]
    for i in range(1, dps):
        first = first + dpbuf[i].astype(F32)
        second = second + g2dp[i]
    gf_ref[...] = first * (1.0 / math.sqrt(nb * ch * dps))
    gs_ref[...] = second[0:lb, 0:nb] * (1.0 / math.sqrt(ch * dps * w))

    own_o.wait()
    wait_back(3, om)
    out_store = pltpu.make_async_copy(om, out_hbm, store_sem.at[3])
    out_store.start()

    @pl.loop(1, n)
    def _(j):
        d = lax.rem(me + j, n)
        copy_to(0, share(u_hbm, d), part(mu, me), d, me).wait_send()
        copy_to(1, part(gac, d), share(gm, me), d, me).wait_send()
        copy_to(2, share(kern, d), part(mk, me), d, me).wait_send()
        copy_to(3, part(oac, d), share(om, me), d, me).wait_send()
        g2_copy(d, me).wait_send()

    for c in halves:
        c.wait_send()
    for j in range(1, dps):
        for c in dp_copies(lax.rem(my_dp + j, dps), my_dp):
            c.wait_send()
    gk_store.wait()
    gi_store.wait()
    gg_store.wait()
    out_store.wait()


def hand_over(*refs):
    for src, dst in zip(refs[:6], refs[6:]):
        dst[...] = src[...]


def on_device(n, dps, inputs, gates, kernel, first_factor, second_factor, upstream):
    lb, ch, w = inputs.shape
    nb = second_factor.shape[0]
    pw = w // (n // (ch // CS))
    owned = w // n
    levels = n.bit_length() - 1
    lanes = max(nb, 128)
    act = jax.ShapeDtypeStruct((lb, ch, w), BF)
    a_act = pltpu.VMEM((lb, ch, w), BF)
    a_mov = pltpu.VMEM((nb, CS, pw), BF)
    hbm = pl.BlockSpec(memory_space=pl.ANY)
    vmem = pl.BlockSpec(memory_space=pltpu.VMEM)
    sem = pltpu.SemaphoreType.DMA
    flops = 6 * lb * ch * w * w
    results = pl.pallas_call(
        functools.partial(layer_kernel, n, dps, lb, ch, w, nb),
        out_shape=(
            act, act, act, act,
            jax.ShapeDtypeStruct((owned, w), F32),
            jax.ShapeDtypeStruct((lb, nb), F32),
        ),
        in_specs=[hbm, hbm, hbm, hbm, vmem, hbm],
        out_specs=(hbm, hbm, hbm, hbm, vmem, vmem),
        scratch_shapes=[
            a_act, a_act, a_act, pltpu.VMEM((w, w), BF),
            a_act, a_act, a_act,
            a_mov, a_mov, a_mov, a_mov,
            a_act, a_act, a_act, a_act, a_act, a_act,
            pltpu.VMEM((nb * CS, nb * CS), BF), pltpu.VMEM((nb * CS, nb * CS), BF),
            pltpu.VMEM((w, w), F32),
            pltpu.VMEM((w, w), BF), pltpu.VMEM((w, w), BF),
            pltpu.VMEM((dps, owned, w), BF),
            pltpu.VMEM((n, 8, lanes), F32), pltpu.VMEM((n, 8, lanes), F32),
            pltpu.VMEM((dps, 8, lanes), F32),
            sem((4,)), sem((4,)), sem((4,)), sem((4, n)), sem((4, n)),
            sem((levels,)), sem((levels,)), sem((n,)), sem((n,)), sem((2, dps)), sem((2, dps)),
        ],
        compiler_params=pltpu.CompilerParams(
            collective_id=0, has_side_effects=True, vmem_limit_bytes=58 * 1024 * 1024
        ),
        cost_estimate=pl.CostEstimate(flops=flops, bytes_accessed=10 << 20, transcendentals=0),
    )(inputs, gates, kernel, first_factor, second_factor, upstream)
    block = pl.BlockSpec((1, ch, w), lambda i: (i, 0, 0))
    specs = [block] * 4 + [pl.BlockSpec(r.shape, lambda i: (0, 0)) for r in results[4:]]
    return pl.pallas_call(
        hand_over,
        grid=(lb,),
        out_shape=tuple(jax.ShapeDtypeStruct(r.shape, r.dtype) for r in results),
        in_specs=specs,
        out_specs=tuple(specs),
        compiler_params=pltpu.CompilerParams(vmem_limit_bytes=60 * 1024 * 1024),
        cost_estimate=pl.CostEstimate(flops=0, bytes_accessed=8 << 20, transcendentals=0),
    )(*results)


def solution(mesh):
    cut = P("seq", "dp", None)
    return jax.shard_map(
        functools.partial(on_device, mesh.shape["seq"], mesh.shape["dp"]),
        mesh=mesh,
        in_specs=(cut, cut, cut, P(), P(), cut),
        out_specs=(cut, cut, cut, cut, P("seq", None), P("seq", None)),
        check_vma=False,
    )
```
